512 devices in a mesh: replica: 16 (over z, x_hi), fsdp: 32 (over x_lo, y, core).
Axes of the slice: x: 4 (x_hi: 2, x_lo: 2; x = x_hi * 2 + x_lo), y: 8, z: 8, core: 2. Of those that a mesh axis runs over, the one named last changes fastest.
Arguments:
- tokens: bfloat16 [131072, 8192], P(('replica', 'fsdp')), may hold values from -6 to 6
- norm_gain: float32 [8192], replicated, may hold values from 0.5 to 1.5
- weights: bfloat16 [16, 8192, 512], P('replica', 'fsdp'), may hold values from -0.0625 to 0.0625
- codes: bfloat16 [16, 8192, 512], P('replica', 'fsdp'), may hold values from -8 to 7, as said below
- scales: float32 [16, 8192, 4], P('replica', 'fsdp'), may hold values from 0.0002 to 0.003
- outer: float32 [8192, 512], P('fsdp', 'replica'), may hold values from -0.0625 to 0.0625
- momentum: float32 [8192, 512], P('fsdp', 'replica'), may hold values from -0.0625 to 0.0625
Outputs:
- keys: bfloat16 [131072, 512], P(('replica', 'fsdp'))
- outer_new: float32 [8192, 512], P('fsdp', 'replica')
- momentum_new: float32 [8192, 512], P('fsdp', 'replica')
- merged: bfloat16 [16, 8192, 512], P('replica', 'fsdp')
The draws below stay inside these ranges and needn't reach their ends.
Inputs may be any that keep to these rules, and one draw needn't show every extreme that they name: `codes`: whole numbers.
All inputs are finite; a program needn't handle non-finite values.
Results may differ from the reference program's by a relative error of at most 0.009.
Values may be sent and summed in bfloat16 or wider, within the bound.
A program may use at most 64 MiB of HBM per device.

```python
import math
import jax
import jax.numpy as jnp
from jax import lax

D = 8192
BLOCK = 128
KC = 512
TOKENS = 131072
N_REPLICA = 16


def draw_codes(key, part):
    key = jax.random.fold_in(key, 7)
    return jax.random.randint(key, (N_REPLICA, D, KC), -8, 8).astype(jnp.bfloat16)


def levels(key, dims, pieces, smallest, high):
    def one(position, shards_of):
        heights = jax.random.uniform(jax.random.fold_in(jax.random.fold_in(key, 6), position), (shards_of,), jnp.float32, smallest / len(pieces), high / len(pieces))
        return jnp.repeat(jnp.exp(heights), dims[position] // shards_of).reshape((-1,) + (1,) * (len(dims) - position - 1))

    gain = one(*pieces[0])
    for cut in pieces[1:]:
        gain = gain * one(*cut)
    return gain


def scatter_about(own_key, shape, width, bound, pieces=(), kind=jnp.bfloat16):
    result = jax.random.normal(own_key, shape, jnp.float32) * width
    if len(pieces) > 0:
        result = levels(own_key, shape, pieces, -0.22, 0.18) * result
    return jnp.clip(result, min=-bound, max=bound).astype(kind)


def setup_inputs(seed: int = 0) -> dict:
    key_list = jax.random.split(jax.random.key(seed), 8)
    tokens = scatter_about(key_list[0], (TOKENS, D), 1.0, 6.0, ((0, 512),))
    norm_gain = jnp.clip(1.0 + 0.1 * jax.random.normal(key_list[1], (D,), jnp.float32), 0.5, 1.5)
    weights = scatter_about(key_list[2], (N_REPLICA, D, KC), D ** -0.5, 0.0625, ((0, 16), (1, 32)))
    codes = draw_codes(jax.random.fold_in(key_list[7], 71), 0)
    scales = jnp.clip(jnp.exp(math.log(0.003) - 2.7080502 * jax.random.uniform(key_list[4], (N_REPLICA, D, KC // BLOCK), jnp.float32) ** levels(key_list[4], (N_REPLICA, D, KC // BLOCK), ((0, 16), (1, 32)), -0.2, 0.2)), 0.0002, 0.003)
    outer = scatter_about(key_list[5], (D, KC), D ** -0.5, 0.0625, ((0, 32), (1, 16)), jnp.float32)
    momentum = scatter_about(key_list[6], (D, KC), 0.004, 0.0625, ((0, 32), (1, 16)), jnp.float32)
    return dict(tokens=tokens, norm_gain=norm_gain, weights=weights, codes=codes, scales=scales, outer=outer, momentum=momentum)


def reference(tokens, norm_gain, weights, codes, scales, outer, momentum):
    values = tokens.astype(jnp.float32)
    stats = lax.optimization_barrier(jnp.mean(values * values, axis=1, keepdims=True))
    normed = (values * lax.rsqrt(stats + 1e-05) * norm_gain).astype(jnp.bfloat16)
    grouped = normed.astype(jnp.float32).reshape(N_REPLICA, TOKENS // N_REPLICA, D)
    keys = jnp.einsum('rtd,rdn->rtn', grouped, weights.astype(jnp.float32), precision=lax.Precision.HIGHEST)
    keys = keys.reshape(TOKENS, KC).astype(jnp.bfloat16)
    blocks = codes.astype(jnp.float32).reshape(N_REPLICA, D, KC // BLOCK, BLOCK)
    total = lax.optimization_barrier(jnp.sum(blocks * scales[:, :, :, None], axis=0)).reshape(D, KC)
    average = total / N_REPLICA
    momentum_new = 0.9 * momentum + average
    outer_new = outer - 0.7 * (average + 0.9 * momentum_new)
    merged = (0.5 * weights.astype(jnp.float32) + 0.5 * outer_new[None]).astype(jnp.bfloat16)
    return (keys, outer_new, momentum_new, merged)
```

```python
import functools

import jax
import jax.numpy as jnp
from jax import lax
from jax.experimental import pallas as pl
from jax.experimental.pallas import tpu as pltpu
from jax.sharding import PartitionSpec as P

BLOCK = 128
LANES = 128
MESH = pl.DeviceIdType.MESH
F32, BF16 = jnp.float32, jnp.bfloat16


def kernel(
    ny, nz, cut,
    tok_hbm, gain_hbm, w_hbm, codes_hbm, scales_hbm, outer_hbm, mom_hbm,
    keys_hbm, outer_out_hbm, mom_out_hbm, merged_hbm,
    tok, gain, codes, scales, outer, mom, keys, merged,
    normed, full, acc, delta, parts, half, avg_blocks,
    local_in, local_out, y_send, y_recv, x_send, x_recv, d_send, d_recv,
    z_send, z_recv, g_send, g_recv, h_send, h_recv,
):
    nk = ny // 2
    rows, columns = full.shape[1], full.shape[2]
    tokens_here, width = tok.shape
    me_r, me_f = lax.axis_index("replica"), lax.axis_index("fsdp")
    z, xh = me_r // 2, me_r % 2
    xl, y, c = me_f // (2 * ny), (me_f // 2) % ny, me_f % 2

    def fsdp(col, row, core):
        return (col * ny + lax.rem(row + 2 * ny, ny)) * 2 + core

    def rep(zz, hh):
        return lax.rem(zz + 2 * nz, nz) * 2 + hh

    up, down = fsdp(xl, y + 1, c), fsdp(xl, y - 1, c)
    across, twin = fsdp(1 - xl, y, c), fsdp(xl, y, 1 - c)

    inputs = [
        pltpu.make_async_copy(w_hbm.at[0], full.at[me_f], local_in.at[0]),
        pltpu.make_async_copy(codes_hbm.at[0], codes, local_in.at[1]),
        pltpu.make_async_copy(scales_hbm, scales, local_in.at[2]),
        pltpu.make_async_copy(outer_hbm, outer, local_in.at[3]),
        pltpu.make_async_copy(mom_hbm, mom, local_in.at[4]),
        pltpu.make_async_copy(gain_hbm, gain, local_in.at[5]),
        pltpu.make_async_copy(tok_hbm, tok, local_in.at[6]),
    ]
    for copy in inputs:
        copy.start()

    barrier = pltpu.get_barrier_semaphore()
    near = [up, down, across, twin]
    far = [rep(z + j, xh) for j in range(1, nz)] + [rep(z, 1 - xh)]
    for other in near:
        pl.semaphore_signal(barrier, inc=1, device_id={"fsdp": other, "replica": me_r}, device_id_type=MESH)
    for other in far:
        pl.semaphore_signal(barrier, inc=1, device_id={"fsdp": me_f, "replica": other}, device_id_type=MESH)
    pl.semaphore_wait(barrier, len(near) + len(far))

    FIRST, SECOND, ALL = (0, cut), (cut, rows - cut), (0, rows)
    EVERY = (0, columns)
    HALF = ((0, columns // 2), (columns // 2, columns // 2))

    def region(owner, rr, cc):
        return full.at[owner, pl.ds(rr[0], rr[1]), pl.ds(cc[0], cc[1])]

    def copy_to(target, owner, rr, cc, send, recv, own=False):
        source = w_hbm.at[0, pl.ds(rr[0], rr[1]), pl.ds(cc[0], cc[1])] if own else region(owner, rr, cc)
        return pltpu.make_async_remote_copy(
            src_ref=source,
            dst_ref=region(owner, rr, cc),
            send_sem=send,
            recv_sem=recv,
            device_id={"fsdp": target, "replica": me_r},
            device_id_type=MESH,
        )

    sent = []

    def start(copy):
        copy.start()
        sent.append(copy)

    toward = (up, down)
    sign = (1, -1)

    def y_copy(d, col, k, part):
        owner = fsdp(col, y - sign[d] * (k - 1), c)
        cc = HALF[d] if k == nk else EVERY
        rr = SECOND if part == 1 else FIRST
        index = (k - 1) * 3 + part
        return copy_to(toward[d], owner, rr, cc, y_send.at[d, index], y_recv.at[d, index], own=(part < 2 and k == 1))

    def y_arrived(d, col, k, part):
        owner = fsdp(col, y - sign[d] * k, c)
        cc = HALF[d] if k == nk else EVERY
        rr = SECOND if part == 1 else FIRST
        index = (k - 1) * 3 + part
        copy_to(toward[d], owner, rr, cc, y_send.at[d, index], y_recv.at[d, index]).wait_recv()

    def x_piece(col, d, k):
        if k == 0:
            return fsdp(col, y, c), (FIRST, SECOND)[d], EVERY, d
        owner = fsdp(col, y - sign[d] * k, c)
        return owner, SECOND, HALF[d] if k == nk else EVERY, 2 * k + d

    def x_copy(d, k):
        owner, rr, cc, index = x_piece(xl, d, k)
        return copy_to(across, owner, rr, cc, x_send.at[index], x_recv.at[index], own=k == 0)

    def x_arrived(d, k):
        owner, rr, cc, index = x_piece(1 - xl, d, k)
        copy_to(across, owner, rr, cc, x_send.at[index], x_recv.at[index]).wait_recv()

    def twin_index(other, d, k):
        return other * ny + (0 if k == 0 else 2 * k - 1 + (d if k < nk else 0))

    def twin_copy(other, d, k):
        col = 1 - xl if other else xl
        index = twin_index(other, d, k)
        return copy_to(twin, fsdp(col, y - sign[d] * k, c), ALL, EVERY, d_send.at[index], d_recv.at[index],
                       own=(other == 0 and k == 0))

    def twin_arrived(other, d, k):
        col = 1 - xl if other else xl
        index = twin_index(other, d, k)
        copy_to(twin, fsdp(col, y - sign[d] * k, 1 - c), ALL, EVERY, d_send.at[index], d_recv.at[index]).wait_recv()

    def multiply(other, k, core, first=False):
        col = 1 - xl if other else xl
        count = 1 if k in (0, nk) else 2

        def one(s, carry):
            owner = fsdp(col, y - (1 - 2 * s) * k, core)
            left = normed[:, pl.ds(pl.multiple_of(owner * rows, rows), rows)]
            product = jnp.dot(left, full[owner], preferred_element_type=F32)
            if first:
                acc[...] = product
            else:
                acc[...] += product
            return carry

        lax.fori_loop(0, count, one, 0)

    for part in (0, 1):
        for d in (0, 1):
            start(y_copy(d, xl, 1, part))
        start(x_copy(part, 0))
    start(twin_copy(0, 0, 0))

    share = columns // nz
    inputs[1].wait()
    inputs[2].wait()
    for b in range(columns // BLOCK):
        block = codes[:, b * BLOCK:(b + 1) * BLOCK].astype(F32).T
        delta[b * BLOCK:(b + 1) * BLOCK, :] = (block * scales[b:b + 1, :]).astype(BF16)
    for j in range(1, nz):
        place = lax.rem(z + j, nz)
        start(pltpu.make_async_remote_copy(
            src_ref=delta.at[pl.ds(place * share, share), :],
            dst_ref=parts.at[j - 1],
            send_sem=z_send.at[j - 1], recv_sem=z_recv.at[j - 1],
            device_id={"fsdp": me_f, "replica": rep(z + j, xh)}, device_id_type=MESH,
        ))

    step_rows = 32
    chunks = width // LANES

    def norm(lo, hi):
        def one(i, carry):
            rr = pl.ds(pl.multiple_of(i * step_rows, step_rows), step_rows)
            squares = jnp.zeros((step_rows, LANES), F32)
            for j in range(chunks):
                v = tok[rr, j * LANES:(j + 1) * LANES].astype(F32)
                squares = squares + v * v
            mean = jnp.sum(squares, axis=1, keepdims=True) * (1.0 / width)
            scale = jnp.broadcast_to(lax.rsqrt(mean + 1e-05), (step_rows, LANES))
            for j in range(chunks):
                v = tok[rr, j * LANES:(j + 1) * LANES].astype(F32)
                normed[rr, j * LANES:(j + 1) * LANES] = (v * scale * gain[j:j + 1, :]).astype(BF16)
            return carry

        lax.fori_loop(lo, hi, one, 0)

    blocks = tokens_here // step_rows
    inputs[5].wait()
    inputs[6].wait()
    inputs[0].wait()
    norm(0, blocks // 2)

    def pass_on(k, part):
        for d in (0, 1):
            y_arrived(d, xl, k, part)
            if k < nk:
                start(y_copy(d, xl, k + 1, part))
        if part == 1:
            for d in (0, 1):
                start(x_copy(d, k))
            for d in (0, 1) if k < nk else (0,):
                start(twin_copy(0, d, k))

    def pass_other(k):
        for d in (0, 1):
            y_arrived(d, 1 - xl, k, 2)
            if k < nk:
                start(y_copy(d, 1 - xl, k + 1, 2))
        for d in (0, 1):
            x_arrived(d, k)
        for d in (0, 1) if k < nk else (0,):
            start(twin_copy(1, d, k))

    def take(other, k):
        for d in (0, 1) if 0 < k < nk else (0,):
            twin_arrived(other, d, k)
        multiply(other, k, 1 - c)

    n_rep = nz * 2
    slim = columns // n_rep

    def outer_sum():
        for j in range(1, nz):
            pltpu.make_async_remote_copy(
                src_ref=parts.at[j - 1], dst_ref=parts.at[j - 1],
                send_sem=z_send.at[j - 1], recv_sem=z_recv.at[j - 1],
                device_id={"fsdp": me_f, "replica": rep(z + j, xh)}, device_id_type=MESH,
            ).wait_recv()

        def total(which):
            lo = pl.multiple_of(z * share + which * slim, slim)
            value = delta[pl.ds(lo, slim), :].astype(F32)
            for j in range(1, nz):
                value = value + parts[j - 1, pl.ds(pl.multiple_of(which * slim, slim), slim), :].astype(F32)
            return value

        half[0] = total(1 - xh).astype(BF16)
        start(half_copy())
        return total(xh)

    def half_copy():
        return pltpu.make_async_remote_copy(
            src_ref=half.at[0], dst_ref=half.at[1], send_sem=h_send.at[0], recv_sem=h_recv.at[0],
            device_id={"fsdp": me_f, "replica": rep(z, 1 - xh)}, device_id_type=MESH,
        )

    def slim_copy(owner):
        ref = avg_blocks.at[pl.ds(pl.multiple_of(owner * slim, slim), slim), :]
        return pltpu.make_async_remote_copy(
            src_ref=ref, dst_ref=ref, send_sem=h_send.at[1], recv_sem=h_recv.at[1],
            device_id={"fsdp": me_f, "replica": rep(z, 1 - xh)}, device_id_type=MESH,
        )

    def share_copy(owner_z, j):
        ref = avg_blocks.at[pl.ds(pl.multiple_of(owner_z * share, share), share), :]
        return pltpu.make_async_remote_copy(
            src_ref=ref, dst_ref=ref, send_sem=g_send.at[j - 1], recv_sem=g_recv.at[j - 1],
            device_id={"fsdp": me_f, "replica": rep(z + j, xh)}, device_id_type=MESH,
        )

    outputs = [
        pltpu.make_async_copy(outer, outer_out_hbm, local_out.at[0]),
        pltpu.make_async_copy(mom, mom_out_hbm, local_out.at[1]),
        pltpu.make_async_copy(merged, merged_hbm.at[0], local_out.at[2]),
        pltpu.make_async_copy(keys, keys_hbm, local_out.at[3]),
    ]

    def outer_step(mine):
        half_copy().wait_recv()
        inputs[3].wait()
        inputs[4].wait()
        average = (mine + half[1].astype(F32)) * (1.0 / n_rep)
        moment = 0.9 * mom[...] + average
        stepped = outer[...] - 0.7 * (average + 0.9 * moment)
        mom[...] = moment
        outer[...] = stepped
        avg_blocks[pl.ds(pl.multiple_of(me_r * slim, slim), slim), :] = stepped.astype(BF16)
        start(slim_copy(me_r))
        outputs[0].start()
        outputs[1].start()

    def outer_spread():
        slim_copy(rep(z, 1 - xh)).wait_recv()
        for j in range(1, nz):
            start(share_copy(z, j))

    def outer_merge():
        for j in range(1, nz):
            share_copy(lax.rem(z - j + nz, nz), j).wait_recv()
        for b in range(columns // LANES):
            block = avg_blocks[b * LANES:(b + 1) * LANES, :].astype(F32).T
            own = full[me_f, :, b * LANES:(b + 1) * LANES].astype(F32)
            merged[:, b * LANES:(b + 1) * LANES] = (0.5 * own + 0.5 * block).astype(BF16)
        outputs[2].start()

    pass_on(1, 0)
    norm(blocks // 2, blocks)
    pass_on(1, 1)
    for part in (0, 1):
        x_arrived(part, 0)
    start(twin_copy(1, 0, 0))
    multiply(0, 0, c, first=True)
    mine = outer_sum()
    multiply(0, 1, c)
    take(0, 0)
    pass_on(2, 0)
    outer_step(mine)
    multiply(1, 0, c)
    take(0, 1)
    outer_spread()
    pass_on(2, 1)
    take(1, 0)
    for k in range(3, nk + 1):
        pass_on(k, 0)
        multiply(0, k - 1, c)
        take(0, k - 1)
        if k == nk:
            for d in (0, 1):
                start(y_copy(d, 1 - xl, 1, 2))
            outer_merge()
        pass_on(k, 1)
    multiply(0, nk, c)
    for k in range(1, nk + 1):
        pass_other(k)
        take(k > 1, max(k - 1, 0) if k > 1 else nk)
        multiply(1, k, c)
    take(1, nk)
    keys[...] = acc[...].astype(BF16)
    outputs[3].start()
    for copy in sent:
        copy.wait_send()
    for copy in outputs:
        copy.wait()


def shards(ny, nz, tokens, norm_gain, weights, codes, scales, outer, momentum):
    tokens_here, width = tokens.shape
    _, rows, columns = weights.shape
    n_fsdp, n_rep = 4 * ny, 2 * nz
    slim, share = columns // n_rep, columns // nz
    nk = ny // 2
    cut = rows * 7 // 16
    anywhere = pl.BlockSpec(memory_space=pl.ANY)
    dma = pltpu.SemaphoreType.DMA
    keys, outer_next, moment_next, merged = pl.pallas_call(
        functools.partial(kernel, ny, nz, cut),
        out_shape=(
            jax.ShapeDtypeStruct((tokens_here, columns), BF16),
            jax.ShapeDtypeStruct((slim, rows), F32),
            jax.ShapeDtypeStruct((slim, rows), F32),
            jax.ShapeDtypeStruct((1, rows, columns), BF16),
        ),
        in_specs=[anywhere] * 7,
        out_specs=(anywhere,) * 4,
        scratch_shapes=[
            pltpu.VMEM((tokens_here, width), BF16),
            pltpu.VMEM((width // LANES, LANES), F32),
            pltpu.VMEM((rows, columns), BF16),
            pltpu.VMEM((columns // BLOCK, rows), F32),
            pltpu.VMEM((slim, rows), F32),
            pltpu.VMEM((slim, rows), F32),
            pltpu.VMEM((tokens_here, columns), BF16),
            pltpu.VMEM((rows, columns), BF16),
            pltpu.VMEM((tokens_here, width), BF16),
            pltpu.VMEM((n_fsdp, rows, columns), BF16),
            pltpu.VMEM((tokens_here, columns), F32),
            pltpu.VMEM((columns, rows), BF16),
            pltpu.VMEM((nz - 1, share, rows), BF16),
            pltpu.VMEM((2, slim, rows), BF16),
            pltpu.VMEM((columns, rows), BF16),
            dma((7,)), dma((4,)),
            dma((2, 3 * nk)), dma((2, 3 * nk)),
            dma((2 * nk + 2,)), dma((2 * nk + 2,)),
            dma((2 * ny,)), dma((2 * ny,)),
            dma((nz - 1,)), dma((nz - 1,)),
            dma((nz - 1,)), dma((nz - 1,)),
            dma((2,)), dma((2,)),
        ],
        compiler_params=pltpu.CompilerParams(
            collective_id=0, has_side_effects=True, vmem_limit_bytes=60 * 1024 * 1024
        ),
        cost_estimate=pl.CostEstimate(
            flops=2 * tokens_here * width * columns, bytes_accessed=2 * tokens_here * width, transcendentals=0
        ),
    )(
        tokens,
        norm_gain.reshape(width // LANES, LANES),
        weights,
        codes,
        scales[0].T,
        outer.T,
        momentum.T,
    )
    return keys, outer_next.T, moment_next.T, merged


def solution(mesh):
    in_specs = (
        P(("replica", "fsdp"), None),
        P(),
        P("replica", "fsdp", None),
        P("replica", "fsdp", None),
        P("replica", "fsdp", None),
        P("fsdp", "replica"),
        P("fsdp", "replica"),
    )
    out_specs = (
        P(("replica", "fsdp"), None),
        P("fsdp", "replica"),
        P("fsdp", "replica"),
        P("replica", "fsdp", None),
    )
    ny, nz = mesh.shape["fsdp"] // 4, mesh.shape["replica"] // 2
    return jax.shard_map(
        functools.partial(shards, ny, nz), mesh=mesh, in_specs=in_specs, out_specs=out_specs, check_vma=False
    )
```

```python
import functools

import jax
import jax.numpy as jnp
from jax import lax
from jax.experimental import pallas as pl
from jax.experimental.pallas import tpu as pltpu
from jax.sharding import PartitionSpec as P

BLOCK = 128
LANES = 128
MESH = pl.DeviceIdType.MESH
F32, BF16 = jnp.float32, jnp.bfloat16


def kernel(
    ny, nz, cut,
    tok_hbm, gain_hbm, w_hbm, codes_hbm, scales_hbm, outer_hbm, mom_hbm,
    keys, outer_out, mom_out, merged,
    tok, gain, codes, scales, outer, mom,
    normed, full, acc, delta, parts, half, avg_blocks,
    local_in, y_send, y_recv, x_send, x_recv, d_send, d_recv,
    z_send, z_recv, g_send, g_recv, h_send, h_recv, near_sem, far_sem,
):
    nk = ny // 2
    rows, columns = full.shape[1], full.shape[2]
    tokens_here, width = tok.shape
    me_r, me_f = lax.axis_index("replica"), lax.axis_index("fsdp")
    z, xh = me_r // 2, me_r % 2
    xl, y, c = me_f // (2 * ny), (me_f // 2) % ny, me_f % 2

    def fsdp(col, row, core):
        return (col * ny + lax.rem(row + 2 * ny, ny)) * 2 + core

    def rep(zz, hh):
        return lax.rem(zz + 2 * nz, nz) * 2 + hh

    up, down = fsdp(xl, y + 1, c), fsdp(xl, y - 1, c)
    across, twin = fsdp(1 - xl, y, c), fsdp(xl, y, 1 - c)

    inputs = [
        pltpu.make_async_copy(w_hbm.at[0], full.at[me_f], local_in.at[0]),
        pltpu.make_async_copy(codes_hbm.at[0], codes, local_in.at[1]),
        pltpu.make_async_copy(scales_hbm, scales, local_in.at[2]),
        pltpu.make_async_copy(outer_hbm, outer, local_in.at[3]),
        pltpu.make_async_copy(mom_hbm, mom, local_in.at[4]),
        pltpu.make_async_copy(gain_hbm, gain, local_in.at[5]),
        pltpu.make_async_copy(tok_hbm, tok, local_in.at[6]),
    ]
    for copy in inputs:
        copy.start()

    barrier = pltpu.get_barrier_semaphore()
    near = [up, down, across, twin]
    far = [rep(z + j, xh) for j in range(1, nz)] + [rep(z, 1 - xh)]
    odd = lax.rem(xl + y + c, 2) == 1
    late = z >= nz // 2

    @pl.when(odd)
    def _():
        for other in near:
            pl.semaphore_signal(barrier, inc=1, device_id={"fsdp": other, "replica": me_r}, device_id_type=MESH)

    @pl.when(jnp.logical_not(odd))
    def _():
        pl.semaphore_wait(barrier, len(near))
        for other in near:
            pl.semaphore_signal(near_sem, inc=1, device_id={"fsdp": other, "replica": me_r}, device_id_type=MESH)

    @pl.when(odd)
    def _():
        pl.semaphore_wait(near_sem, len(near))
        for other in far:
            pl.semaphore_signal(barrier, inc=1, device_id={"fsdp": me_f, "replica": other}, device_id_type=MESH)

    def meet_far():
        @pl.when(odd)
        def _():
            pl.semaphore_wait(barrier, len(far))
            pl.semaphore_signal(far_sem, inc=1, device_id={"fsdp": twin, "replica": me_r}, device_id_type=MESH)

        @pl.when(jnp.logical_not(odd))
        def _():
            pl.semaphore_wait(far_sem, 1)

    FIRST, SECOND, ALL = (0, cut), (cut, rows - cut), (0, rows)
    EVERY = (0, columns)
    HALF = ((0, columns // 2), (columns // 2, columns // 2))

    def region(owner, rr, cc):
        return full.at[owner, pl.ds(rr[0], rr[1]), pl.ds(cc[0], cc[1])]

    def copy_to(target, owner, rr, cc, send, recv, own=False):
        source = w_hbm.at[0, pl.ds(rr[0], rr[1]), pl.ds(cc[0], cc[1])] if own else region(owner, rr, cc)
        return pltpu.make_async_remote_copy(
            src_ref=source,
            dst_ref=region(owner, rr, cc),
            send_sem=send,
            recv_sem=recv,
            device_id={"fsdp": target, "replica": me_r},
            device_id_type=MESH,
        )

    sent = []

    def start(copy):
        copy.start()
        sent.append(copy)

    toward = (up, down)
    sign = (1, -1)

    def y_copy(d, col, k, part):
        owner = fsdp(col, y - sign[d] * (k - 1), c)
        cc = HALF[d] if k == nk else EVERY
        rr = SECOND if part == 1 else FIRST
        index = (k - 1) * 3 + part
        return copy_to(toward[d], owner, rr, cc, y_send.at[d, index], y_recv.at[d, index], own=(part < 2 and k == 1))

    def y_arrived(d, col, k, part):
        owner = fsdp(col, y - sign[d] * k, c)
        cc = HALF[d] if k == nk else EVERY
        rr = SECOND if part == 1 else FIRST
        index = (k - 1) * 3 + part
        copy_to(toward[d], owner, rr, cc, y_send.at[d, index], y_recv.at[d, index]).wait_recv()

    def x_piece(col, d, k):
        if k == 0:
            return fsdp(col, y, c), (FIRST, SECOND)[d], EVERY, d
        owner = fsdp(col, y - sign[d] * k, c)
        return owner, SECOND, HALF[d] if k == nk else EVERY, 2 * k + d

    def x_copy(d, k):
        owner, rr, cc, index = x_piece(xl, d, k)
        return copy_to(across, owner, rr, cc, x_send.at[index], x_recv.at[index], own=k == 0)

    def x_arrived(d, k):
        owner, rr, cc, index = x_piece(1 - xl, d, k)
        copy_to(across, owner, rr, cc, x_send.at[index], x_recv.at[index]).wait_recv()

    def twin_index(other, d, k):
        return other * ny + (0 if k == 0 else 2 * k - 1 + (d if k < nk else 0))

    def twin_copy(other, d, k):
        col = 1 - xl if other else xl
        index = twin_index(other, d, k)
        return copy_to(twin, fsdp(col, y - sign[d] * k, c), ALL, EVERY, d_send.at[index], d_recv.at[index],
                       own=(other == 0 and k == 0))

    def twin_arrived(other, d, k):
        col = 1 - xl if other else xl
        index = twin_index(other, d, k)
        copy_to(twin, fsdp(col, y - sign[d] * k, 1 - c), ALL, EVERY, d_send.at[index], d_recv.at[index]).wait_recv()

    def multiply(other, k, core, first=False):
        col = 1 - xl if other else xl
        count = 1 if k in (0, nk) else 2

        def one(s, carry):
            owner = fsdp(col, y - (1 - 2 * s) * k, core)
            left = normed[:, pl.ds(pl.multiple_of(owner * rows, rows), rows)]
            product = jnp.dot(left, full[owner], preferred_element_type=F32)
            if first:
                acc[...] = product
            else:
                acc[...] += product
            return carry

        lax.fori_loop(0, count, one, 0)

    for part in (0, 1):
        for d in (0, 1):
            start(y_copy(d, xl, 1, part))
        start(x_copy(part, 0))
    start(twin_copy(0, 0, 0))

    share = columns // nz
    inputs[1].wait()
    inputs[2].wait()
    for b in range(columns // BLOCK):
        block = codes[:, b * BLOCK:(b + 1) * BLOCK].astype(F32).T
        delta[b * BLOCK:(b + 1) * BLOCK, :] = (block * scales[b:b + 1, :]).astype(BF16)
    reduce_copies = [
        pltpu.make_async_remote_copy(
            src_ref=delta.at[pl.ds(pl.multiple_of(lax.rem(z + j, nz) * share, share), share), :],
            dst_ref=parts.at[j - 1],
            send_sem=z_send.at[j - 1], recv_sem=z_recv.at[j - 1],
            device_id={"fsdp": me_f, "replica": rep(z + j, xh)}, device_id_type=MESH,
        )
        for j in range(1, nz)
    ]
    sent.extend(reduce_copies)

    def outer_send():
        meet_far()
        for copy in reduce_copies:
            copy.start()

    pl.when(late)(outer_send)

    step_rows = 32
    chunks = width // LANES

    def norm(lo, hi):
        def one(i, carry):
            rr = pl.ds(pl.multiple_of(i * step_rows, step_rows), step_rows)
            squares = jnp.zeros((step_rows, LANES), F32)
            for j in range(chunks):
                v = tok[rr, j * LANES:(j + 1) * LANES].astype(F32)
                squares = squares + v * v
            mean = jnp.sum(squares, axis=1, keepdims=True) * (1.0 / width)
            scale = jnp.broadcast_to(lax.rsqrt(mean + 1e-05), (step_rows, LANES))
            for j in range(chunks):
                v = tok[rr, j * LANES:(j + 1) * LANES].astype(F32)
                normed[rr, j * LANES:(j + 1) * LANES] = (v * scale * gain[j:j + 1, :]).astype(BF16)
            return carry

        lax.fori_loop(lo, hi, one, 0)

    blocks = tokens_here // step_rows
    inputs[5].wait()
    inputs[6].wait()
    inputs[0].wait()
    norm(0, blocks // 2)

    def ways(k):
        return (0, 1) if k < nk else (0,)

    def pass_own(k):
        for part in (0, 1):
            for d in (0, 1):
                y_arrived(d, xl, k, part)
                if k < nk:
                    start(y_copy(d, xl, k + 1, part))
        for d in (0, 1):
            start(x_copy(d, k))
        for d in ways(k):
            start(twin_copy(0, d, k))

    def pass_first(k):
        for d in (0, 1):
            if k == 0:
                start(y_copy(d, 1 - xl, 1, 2))
            else:
                y_arrived(d, 1 - xl, k, 2)
                if k < nk:
                    start(y_copy(d, 1 - xl, k + 1, 2))

    def complete(k):
        for d in (0, 1):
            x_arrived(d, k)
        for d in ways(k):
            start(twin_copy(1, d, k))

    def take(other, k):
        for d in ways(k) if k else (0,):
            twin_arrived(other, d, k)
        multiply(other, k, 1 - c)

    n_rep = nz * 2
    slim = columns // n_rep

    def outer_sum():
        for j in range(1, nz):
            pltpu.make_async_remote_copy(
                src_ref=parts.at[j - 1], dst_ref=parts.at[j - 1],
                send_sem=z_send.at[j - 1], recv_sem=z_recv.at[j - 1],
                device_id={"fsdp": me_f, "replica": rep(z + j, xh)}, device_id_type=MESH,
            ).wait_recv()

        def total(which):
            lo = pl.multiple_of(z * share + which * slim, slim)
            value = delta[pl.ds(lo, slim), :].astype(F32)
            for j in range(1, nz):
                value = value + parts[j - 1, pl.ds(pl.multiple_of(which * slim, slim), slim), :].astype(F32)
            return value

        half[0] = total(1 - xh).astype(BF16)
        start(half_copy())
        return total(xh)

    def half_copy():
        return pltpu.make_async_remote_copy(
            src_ref=half.at[0], dst_ref=half.at[1], send_sem=h_send.at[0], recv_sem=h_recv.at[0],
            device_id={"fsdp": me_f, "replica": rep(z, 1 - xh)}, device_id_type=MESH,
        )

    def slim_copy(owner):
        ref = avg_blocks.at[pl.ds(pl.multiple_of(owner * slim, slim), slim), :]
        return pltpu.make_async_remote_copy(
            src_ref=ref, dst_ref=ref, send_sem=h_send.at[1], recv_sem=h_recv.at[1],
            device_id={"fsdp": me_f, "replica": rep(z, 1 - xh)}, device_id_type=MESH,
        )

    def share_copy(owner_z, j):
        ref = avg_blocks.at[pl.ds(pl.multiple_of(owner_z * share, share), share), :]
        return pltpu.make_async_remote_copy(
            src_ref=ref, dst_ref=ref, send_sem=g_send.at[j - 1], recv_sem=g_recv.at[j - 1],
            device_id={"fsdp": me_f, "replica": rep(z + j, xh)}, device_id_type=MESH,
        )

    def outer_step(mine):
        half_copy().wait_recv()
        inputs[3].wait()
        inputs[4].wait()
        average = (mine + half[1].astype(F32)) * (1.0 / n_rep)
        moment = 0.9 * mom[...] + average
        stepped = outer[...] - 0.7 * (average + 0.9 * moment)
        mom_out[...] = moment
        outer_out[...] = stepped
        avg_blocks[pl.ds(pl.multiple_of(me_r * slim, slim), slim), :] = stepped.astype(BF16)
        start(slim_copy(me_r))

    spread_copies = [share_copy(z, j) for j in range(1, nz)]

    def outer_spread():
        slim_copy(rep(z, 1 - xh)).wait_recv()
        for copy in spread_copies:
            copy.start()

    def outer_merge():
        for j in range(1, nz):
            share_copy(lax.rem(z - j + nz, nz), j).wait_recv()
        for b in range(columns // LANES):
            block = avg_blocks[b * LANES:(b + 1) * LANES, :].astype(F32).T
            own = full[me_f, :, b * LANES:(b + 1) * LANES].astype(F32)
            merged[0, :, b * LANES:(b + 1) * LANES] = (0.5 * own + 0.5 * block).astype(BF16)

    pass_own(1)
    pl.when(jnp.logical_not(late))(outer_send)
    norm(blocks // 2, blocks)
    x_arrived(0, 0)
    x_arrived(1, 0)
    start(twin_copy(1, 0, 0))
    multiply(0, 0, c, first=True)
    take(0, 0)
    pass_own(2)
    pass_first(0)
    mine = outer_sum()
    multiply(0, 1, c)
    multiply(1, 0, c)
    take(0, 1)
    outer_step(mine)
    take(1, 0)
    pl.when(late)(outer_spread)
    pass_own(3)
    sent.extend(spread_copies)
    pl.when(jnp.logical_not(late))(outer_spread)
    multiply(0, 2, c)
    take(0, 2)
    pass_first(1)
    multiply(0, 3, c)
    pass_own(4)
    take(0, 3)
    pass_first(2)
    complete(1)
    multiply(0, 4, c)
    multiply(1, 1, c)
    take(0, 4)
    pass_first(3)
    complete(2)
    multiply(1, 2, c)
    take(1, 1)
    complete(3)
    multiply(1, 3, c)
    take(1, 2)
    outer_merge()
    take(1, 3)
    pass_first(4)
    complete(4)
    multiply(1, 4, c)
    take(1, 4)
    keys[...] = acc[...].astype(BF16)
    for copy in sent:
        copy.wait_send()


def write(keys, outer, mom, merged, keys_out, outer_out, mom_out, merged_out, sems):
    pairs = ((keys, keys_out), (outer, outer_out), (mom, mom_out), (merged, merged_out))
    copies = [pltpu.make_async_copy(a, b, sems.at[i]) for i, (a, b) in enumerate(pairs)]
    for copy in copies:
        copy.start()
    for copy in copies:
        copy.wait()


def shards(ny, nz, tokens, norm_gain, weights, codes, scales, outer, momentum):
    tokens_here, width = tokens.shape
    _, rows, columns = weights.shape
    n_fsdp, n_rep = 4 * ny, 2 * nz
    slim, share = columns // n_rep, columns // nz
    nk = ny // 2
    cut = rows // 2
    hbm = pl.BlockSpec(memory_space=pltpu.HBM)
    vmem = pl.BlockSpec(memory_space=pltpu.VMEM)
    dma = pltpu.SemaphoreType.DMA
    results = (
        ((tokens_here, columns), BF16),
        ((slim, rows), F32),
        ((slim, rows), F32),
        ((1, rows, columns), BF16),
    )
    held = pl.pallas_call(
        functools.partial(kernel, ny, nz, cut),
        out_shape=tuple(pltpu.VMEM(shape, dtype) for shape, dtype in results),
        in_specs=[hbm] * 7,
        out_specs=(vmem,) * 4,
        scratch_shapes=[
            pltpu.VMEM((tokens_here, width), BF16),
            pltpu.VMEM((width // LANES, LANES), F32),
            pltpu.VMEM((rows, columns), BF16),
            pltpu.VMEM((columns // BLOCK, rows), F32),
            pltpu.VMEM((slim, rows), F32),
            pltpu.VMEM((slim, rows), F32),
            pltpu.VMEM((tokens_here, width), BF16),
            pltpu.VMEM((n_fsdp, rows, columns), BF16),
            pltpu.VMEM((tokens_here, columns), F32),
            pltpu.VMEM((columns, rows), BF16),
            pltpu.VMEM((nz - 1, share, rows), BF16),
            pltpu.VMEM((2, slim, rows), BF16),
            pltpu.VMEM((columns, rows), BF16),
            dma((7,)),
            dma((2, 3 * nk)), dma((2, 3 * nk)),
            dma((2 * nk + 2,)), dma((2 * nk + 2,)),
            dma((2 * ny,)), dma((2 * ny,)),
            dma((nz - 1,)), dma((nz - 1,)),
            dma((nz - 1,)), dma((nz - 1,)),
            dma((2,)), dma((2,)),
            pltpu.SemaphoreType.REGULAR, pltpu.SemaphoreType.REGULAR,
        ],
        compiler_params=pltpu.CompilerParams(
            collective_id=0, has_side_effects=True, vmem_limit_bytes=60 * 1024 * 1024
        ),
        cost_estimate=pl.CostEstimate(
            flops=2 * tokens_here * width * columns, bytes_accessed=2 * tokens_here * width, transcendentals=0
        ),
    )(
        tokens,
        norm_gain.reshape(width // LANES, LANES),
        weights,
        codes,
        scales[0].T,
        outer.T,
        momentum.T,
    )
    keys, outer_next, moment_next, merged = pl.pallas_call(
        write,
        out_shape=tuple(jax.ShapeDtypeStruct(shape, dtype) for shape, dtype in results),
        in_specs=[vmem] * 4,
        out_specs=(hbm,) * 4,
        scratch_shapes=[dma((4,))],
        compiler_params=pltpu.CompilerParams(vmem_limit_bytes=4 * 1024 * 1024),
    )(*held)
    return keys, outer_next.T, moment_next.T, merged


def solution(mesh):
    in_specs = (
        P(("replica", "fsdp"), None),
        P(),
        P("replica", "fsdp", None),
        P("replica", "fsdp", None),
        P("replica", "fsdp", None),
        P("fsdp", "replica"),
        P("fsdp", "replica"),
    )
    out_specs = (
        P(("replica", "fsdp"), None),
        P("fsdp", "replica"),
        P("fsdp", "replica"),
        P("replica", "fsdp", None),
    )
    ny, nz = mesh.shape["fsdp"] // 4, mesh.shape["replica"] // 2
    return jax.shard_map(
        functools.partial(shards, ny, nz), mesh=mesh, in_specs=in_specs, out_specs=out_specs, check_vma=False
    )
```

```python
import functools

import jax
import jax.numpy as jnp
from jax import lax
from jax.experimental import pallas as pl
from jax.experimental.pallas import tpu as pltpu
from jax.sharding import PartitionSpec as P

BLOCK = 128
LANES = 128
MESH = pl.DeviceIdType.MESH
ORDER = (
    "l0", "n0", "G1", "F1", "T1", "e0", "P0", "n1", "X0", "M0", "t0", "l1",
    "G2", "F2", "T2", "P1", "e1", "l2", "M1", "N0", "t1", "e2", "x0", "l3",
    "G3", "P2", "F3", "T3", "e3", "M2", "t2", "M3", "G4", "X1", "F4", "T4",
    "t3", "P3", "M4", "N1", "t4", "X2", "N2", "x1", "X3", "N3", "x2", "P4",
    "X4", "Z0", "N4", "x3", "x4",
)
F32, BF16 = jnp.float32, jnp.bfloat16


def kernel(
    ny, nz, cut,
    tok_hbm, gain_hbm, w_hbm, codes_hbm, scales_hbm, outer_hbm, mom_hbm,
    keys, outer_out, mom_out, merged,
    tok, gain, codes, scales, outer, mom,
    normed, full, acc, delta, parts, half, avg_blocks, mine,
    local_in, y_send, y_recv, x_send, x_recv, d_send, d_recv,
    z_send, z_recv, g_send, g_recv, h_send, h_recv, near_sem, far_sem,
):
    nk = ny // 2
    rows, columns = full.shape[1], full.shape[2]
    tokens_here, width = tok.shape
    me_r, me_f = lax.axis_index("replica"), lax.axis_index("fsdp")
    z, xh = me_r // 2, me_r % 2
    xl, y, c = me_f // (2 * ny), (me_f // 2) % ny, me_f % 2

    def fsdp(col, row, core):
        return (col * ny + lax.rem(row + 2 * ny, ny)) * 2 + core

    def rep(zz, hh):
        return lax.rem(zz + 2 * nz, nz) * 2 + hh

    up, down = fsdp(xl, y + 1, c), fsdp(xl, y - 1, c)
    across, twin = fsdp(1 - xl, y, c), fsdp(xl, y, 1 - c)

    inputs = [
        pltpu.make_async_copy(w_hbm.at[0], full.at[me_f], local_in.at[0]),
        pltpu.make_async_copy(codes_hbm.at[0], codes, local_in.at[1]),
        pltpu.make_async_copy(scales_hbm, scales, local_in.at[2]),
        pltpu.make_async_copy(outer_hbm, outer, local_in.at[3]),
        pltpu.make_async_copy(mom_hbm, mom, local_in.at[4]),
        pltpu.make_async_copy(gain_hbm, gain, local_in.at[5]),
        pltpu.make_async_copy(tok_hbm, tok, local_in.at[6]),
    ]
    for copy in inputs:
        copy.start()

    barrier = pltpu.get_barrier_semaphore()
    near = [up, down, across, twin]
    far = [rep(z + j, xh) for j in range(1, nz)] + [rep(z, 1 - xh)]
    odd = lax.rem(xl + y + c, 2) == 1
    late = z >= nz // 2

    @pl.when(odd)
    def _():
        for other in near:
            pl.semaphore_signal(barrier, inc=1, device_id={"fsdp": other, "replica": me_r}, device_id_type=MESH)

    @pl.when(jnp.logical_not(odd))
    def _():
        pl.semaphore_wait(barrier, len(near))
        for other in near:
            pl.semaphore_signal(near_sem, inc=1, device_id={"fsdp": other, "replica": me_r}, device_id_type=MESH)

    @pl.when(odd)
    def _():
        pl.semaphore_wait(near_sem, len(near))
        for other in far:
            pl.semaphore_signal(barrier, inc=1, device_id={"fsdp": me_f, "replica": other}, device_id_type=MESH)

    def meet_far():
        @pl.when(odd)
        def _():
            pl.semaphore_wait(barrier, len(far))
            pl.semaphore_signal(far_sem, inc=1, device_id={"fsdp": twin, "replica": me_r}, device_id_type=MESH)

        @pl.when(jnp.logical_not(odd))
        def _():
            pl.semaphore_wait(far_sem, 1)

    FIRST, SECOND, ALL = (0, cut), (cut, rows - cut), (0, rows)
    EVERY = (0, columns)
    HALF = ((0, columns // 2), (columns // 2, columns // 2))

    def region(owner, rr, cc):
        return full.at[owner, pl.ds(rr[0], rr[1]), pl.ds(cc[0], cc[1])]

    def copy_to(target, owner, rr, cc, send, recv, own=False):
        source = w_hbm.at[0, pl.ds(rr[0], rr[1]), pl.ds(cc[0], cc[1])] if own else region(owner, rr, cc)
        return pltpu.make_async_remote_copy(
            src_ref=source,
            dst_ref=region(owner, rr, cc),
            send_sem=send,
            recv_sem=recv,
            device_id={"fsdp": target, "replica": me_r},
            device_id_type=MESH,
        )

    sent = []

    def start(copy):
        copy.start()
        sent.append(copy)

    toward = (up, down)
    sign = (1, -1)

    def y_copy(d, col, k, part):
        owner = fsdp(col, y - sign[d] * (k - 1), c)
        cc = HALF[d] if k == nk else EVERY
        rr = SECOND if part == 1 else FIRST
        index = (k - 1) * 3 + part
        return copy_to(toward[d], owner, rr, cc, y_send.at[d, index], y_recv.at[d, index], own=(part < 2 and k == 1))

    def y_arrived(d, col, k, part):
        owner = fsdp(col, y - sign[d] * k, c)
        cc = HALF[d] if k == nk else EVERY
        rr = SECOND if part == 1 else FIRST
        index = (k - 1) * 3 + part
        copy_to(toward[d], owner, rr, cc, y_send.at[d, index], y_recv.at[d, index]).wait_recv()

    def x_piece(col, d, k):
        if k == 0:
            return fsdp(col, y, c), (FIRST, SECOND)[d], EVERY, d
        owner = fsdp(col, y - sign[d] * k, c)
        return owner, SECOND, HALF[d] if k == nk else EVERY, 2 * k + d

    def x_copy(d, k):
        owner, rr, cc, index = x_piece(xl, d, k)
        return copy_to(across, owner, rr, cc, x_send.at[index], x_recv.at[index], own=k == 0)

    def x_arrived(d, k):
        owner, rr, cc, index = x_piece(1 - xl, d, k)
        copy_to(across, owner, rr, cc, x_send.at[index], x_recv.at[index]).wait_recv()

    def twin_index(other, d, k):
        return other * ny + (0 if k == 0 else 2 * k - 1 + (d if k < nk else 0))

    def twin_copy(other, d, k):
        col = 1 - xl if other else xl
        index = twin_index(other, d, k)
        return copy_to(twin, fsdp(col, y - sign[d] * k, c), ALL, EVERY, d_send.at[index], d_recv.at[index],
                       own=(other == 0 and k == 0))

    def twin_arrived(other, d, k):
        col = 1 - xl if other else xl
        index = twin_index(other, d, k)
        copy_to(twin, fsdp(col, y - sign[d] * k, 1 - c), ALL, EVERY, d_send.at[index], d_recv.at[index]).wait_recv()

    def multiply(other, k, core, first=False):
        col = 1 - xl if other else xl
        count = 1 if k in (0, nk) else 2

        def one(s, carry):
            owner = fsdp(col, y - (1 - 2 * s) * k, core)
            left = normed[:, pl.ds(pl.multiple_of(owner * rows, rows), rows)]
            product = jnp.dot(left, full[owner], preferred_element_type=F32)
            if first:
                acc[...] = product
            else:
                acc[...] += product
            return carry

        lax.fori_loop(0, count, one, 0)

    start(x_copy(0, 0))
    for d in (0, 1):
        start(y_copy(d, xl, 1, 1))
    for d in (0, 1):
        start(y_copy(d, xl, 1, 0))
    start(x_copy(1, 0))
    start(twin_copy(0, 0, 0))

    share = columns // nz
    inputs[1].wait()
    inputs[2].wait()
    for b in range(columns // BLOCK):
        block = codes[:, b * BLOCK:(b + 1) * BLOCK].astype(F32).T
        delta[b * BLOCK:(b + 1) * BLOCK, :] = (block * scales[b:b + 1, :]).astype(BF16)
    reduce_copies = [
        pltpu.make_async_remote_copy(
            src_ref=delta.at[pl.ds(pl.multiple_of(lax.rem(z + j, nz) * share, share), share), :],
            dst_ref=parts.at[j - 1],
            send_sem=z_send.at[j - 1], recv_sem=z_recv.at[j - 1],
            device_id={"fsdp": me_f, "replica": rep(z + j, xh)}, device_id_type=MESH,
        )
        for j in range(1, nz)
    ]
    sent.extend(reduce_copies)

    def outer_send():
        meet_far()
        for copy in reduce_copies:
            copy.start()


    step_rows = 32
    chunks = width // LANES

    def norm(lo, hi):
        def one(i, carry):
            rr = pl.ds(pl.multiple_of(i * step_rows, step_rows), step_rows)
            squares = jnp.zeros((step_rows, LANES), F32)
            for j in range(chunks):
                v = tok[rr, j * LANES:(j + 1) * LANES].astype(F32)
                squares = squares + v * v
            mean = jnp.sum(squares, axis=1, keepdims=True) * (1.0 / width)
            scale = jnp.broadcast_to(lax.rsqrt(mean + 1e-05), (step_rows, LANES))
            for j in range(chunks):
                v = tok[rr, j * LANES:(j + 1) * LANES].astype(F32)
                normed[rr, j * LANES:(j + 1) * LANES] = (v * scale * gain[j:j + 1, :]).astype(BF16)
            return carry

        lax.fori_loop(lo, hi, one, 0)

    blocks = tokens_here // step_rows
    inputs[3].wait()
    inputs[4].wait()
    inputs[5].wait()
    inputs[6].wait()
    inputs[0].wait()
    def ways(k):
        return (0, 1) if k < nk else (0,)

    def pass_own(k, part):
        for d in (0, 1):
            y_arrived(d, xl, k, part)
            if k < nk:
                start(y_copy(d, xl, k + 1, part))
        if part == 1:
            for d in (0, 1):
                start(x_copy(d, k))

    def own_to_twin(k):
        for d in ways(k):
            start(twin_copy(0, d, k))

    def pass_first(k):
        for d in (0, 1):
            if k == 0:
                if d == 0:
                    x_arrived(0, 0)
                start(y_copy(d, 1 - xl, 1, 2))
            else:
                y_arrived(d, 1 - xl, k, 2)
                if k < nk:
                    start(y_copy(d, 1 - xl, k + 1, 2))

    def complete(k):
        for d in (0, 1) if k else (1,):
            x_arrived(d, k)
        for d in ways(k) if k else (0,):
            start(twin_copy(1, d, k))

    def take(other, k):
        for d in ways(k) if k else (0,):
            twin_arrived(other, d, k)
        multiply(other, k, 1 - c)

    n_rep = nz * 2
    slim = columns // n_rep

    def outer_sum():
        for j in range(1, nz):
            pltpu.make_async_remote_copy(
                src_ref=parts.at[j - 1], dst_ref=parts.at[j - 1],
                send_sem=z_send.at[j - 1], recv_sem=z_recv.at[j - 1],
                device_id={"fsdp": me_f, "replica": rep(z + j, xh)}, device_id_type=MESH,
            ).wait_recv()

        def total(which):
            lo = pl.multiple_of(z * share + which * slim, slim)
            value = delta[pl.ds(lo, slim), :].astype(F32)
            for j in range(1, nz):
                value = value + parts[j - 1, pl.ds(pl.multiple_of(which * slim, slim), slim), :].astype(F32)
            return value

        half[0] = total(1 - xh).astype(BF16)
        half_copy().start()
        mine[...] = total(xh)

    def half_copy():
        return pltpu.make_async_remote_copy(
            src_ref=half.at[0], dst_ref=half.at[1], send_sem=h_send.at[0], recv_sem=h_recv.at[0],
            device_id={"fsdp": me_f, "replica": rep(z, 1 - xh)}, device_id_type=MESH,
        )

    def slim_copy(owner):
        ref = avg_blocks.at[pl.ds(pl.multiple_of(owner * slim, slim), slim), :]
        return pltpu.make_async_remote_copy(
            src_ref=ref, dst_ref=ref, send_sem=h_send.at[1], recv_sem=h_recv.at[1],
            device_id={"fsdp": me_f, "replica": rep(z, 1 - xh)}, device_id_type=MESH,
        )

    def share_copy(owner_z, j):
        ref = avg_blocks.at[pl.ds(pl.multiple_of(owner_z * share, share), share), :]
        return pltpu.make_async_remote_copy(
            src_ref=ref, dst_ref=ref, send_sem=g_send.at[j - 1], recv_sem=g_recv.at[j - 1],
            device_id={"fsdp": me_f, "replica": rep(z + j, xh)}, device_id_type=MESH,
        )

    slim_out = slim_copy(me_r)
    sent.extend([half_copy(), slim_out])

    def outer_step():
        half_copy().wait_recv()
        average = (mine[...] + half[1].astype(F32)) * (1.0 / n_rep)
        moment = 0.9 * mom[...] + average
        stepped = outer[...] - 0.7 * (average + 0.9 * moment)
        mom_out[...] = moment
        outer_out[...] = stepped
        avg_blocks[pl.ds(pl.multiple_of(me_r * slim, slim), slim), :] = stepped.astype(BF16)
        slim_out.start()

    spread_copies = [share_copy(z, j) for j in range(1, nz)]

    def outer_spread():
        slim_copy(rep(z, 1 - xh)).wait_recv()
        for copy in spread_copies:
            copy.start()

    def outer_merge():
        for j in range(1, nz):
            share_copy(lax.rem(z - j + nz, nz), j).wait_recv()
        for b in range(columns // LANES):
            block = avg_blocks[b * LANES:(b + 1) * LANES, :].astype(F32).T
            own = full[me_f, :, b * LANES:(b + 1) * LANES].astype(F32)
            merged[0, :, b * LANES:(b + 1) * LANES] = (0.5 * own + 0.5 * block).astype(BF16)

    early = jnp.logical_not(late)
    steps = {
        "F": lambda k: pass_own(k, 0),
        "G": lambda k: pass_own(k, 1),
        "T": own_to_twin,
        "P": pass_first,
        "X": complete,
        "M": lambda k: multiply(0, k, c, first=k == 0),
        "N": lambda k: multiply(1, k, c),
        "t": lambda k: take(0, k),
        "x": lambda k: take(1, k),
        "n": lambda k: norm(blocks * k // 2, blocks * (k + 1) // 2),
        "e": lambda k: pl.when(early)((outer_send, outer_sum, outer_step, outer_spread)[k]),
        "l": lambda k: pl.when(late)((outer_send, outer_sum, outer_step, outer_spread)[k]),
        "Z": lambda k: outer_merge(),
    }
    for step in ORDER:
        steps[step[0]](int(step[1]))
    sent.extend(spread_copies)
    keys[...] = acc[...].astype(BF16)
    for copy in sent:
        copy.wait_send()


def write(keys, outer, mom, merged, keys_out, outer_out, mom_out, merged_out, sems):
    pairs = ((keys, keys_out), (outer, outer_out), (mom, mom_out), (merged, merged_out))
    copies = [pltpu.make_async_copy(a, b, sems.at[i]) for i, (a, b) in enumerate(pairs)]
    for copy in copies:
        copy.start()
    for copy in copies:
        copy.wait()


def shards(ny, nz, tokens, norm_gain, weights, codes, scales, outer, momentum):
    tokens_here, width = tokens.shape
    _, rows, columns = weights.shape
    n_fsdp, n_rep = 4 * ny, 2 * nz
    slim, share = columns // n_rep, columns // nz
    nk = ny // 2
    cut = rows * 7 // 16
    hbm = pl.BlockSpec(memory_space=pltpu.HBM)
    vmem = pl.BlockSpec(memory_space=pltpu.VMEM)
    dma = pltpu.SemaphoreType.DMA
    results = (
        ((tokens_here, columns), BF16),
        ((slim, rows), F32),
        ((slim, rows), F32),
        ((1, rows, columns), BF16),
    )
    held = pl.pallas_call(
        functools.partial(kernel, ny, nz, cut),
        out_shape=tuple(pltpu.VMEM(shape, dtype) for shape, dtype in results),
        in_specs=[hbm] * 7,
        out_specs=(vmem,) * 4,
        scratch_shapes=[
            pltpu.VMEM((tokens_here, width), BF16),
            pltpu.VMEM((width // LANES, LANES), F32),
            pltpu.VMEM((rows, columns), BF16),
            pltpu.VMEM((columns // BLOCK, rows), F32),
            pltpu.VMEM((slim, rows), F32),
            pltpu.VMEM((slim, rows), F32),
            pltpu.VMEM((tokens_here, width), BF16),
            pltpu.VMEM((n_fsdp, rows, columns), BF16),
            pltpu.VMEM((tokens_here, columns), F32),
            pltpu.VMEM((columns, rows), BF16),
            pltpu.VMEM((nz - 1, share, rows), BF16),
            pltpu.VMEM((2, slim, rows), BF16),
            pltpu.VMEM((columns, rows), BF16),
            pltpu.VMEM((slim, rows), F32),
            dma((7,)),
            dma((2, 3 * nk)), dma((2, 3 * nk)),
            dma((2 * nk + 2,)), dma((2 * nk + 2,)),
            dma((2 * ny,)), dma((2 * ny,)),
            dma((nz - 1,)), dma((nz - 1,)),
            dma((nz - 1,)), dma((nz - 1,)),
            dma((2,)), dma((2,)),
            pltpu.SemaphoreType.REGULAR, pltpu.SemaphoreType.REGULAR,
        ],
        compiler_params=pltpu.CompilerParams(
            collective_id=0, has_side_effects=True, vmem_limit_bytes=60 * 1024 * 1024
        ),
        cost_estimate=pl.CostEstimate(
            flops=2 * tokens_here * width * columns, bytes_accessed=2 * tokens_here * width, transcendentals=0
        ),
    )(
        tokens,
        norm_gain.reshape(width // LANES, LANES),
        weights,
        codes,
        scales[0].T,
        outer.T,
        momentum.T,
    )
    keys, outer_next, moment_next, merged = pl.pallas_call(
        write,
        out_shape=tuple(jax.ShapeDtypeStruct(shape, dtype) for shape, dtype in results),
        in_specs=[vmem] * 4,
        out_specs=(hbm,) * 4,
        scratch_shapes=[dma((4,))],
        compiler_params=pltpu.CompilerParams(vmem_limit_bytes=4 * 1024 * 1024),
    )(*held)
    return keys, outer_next.T, moment_next.T, merged


def solution(mesh):
    in_specs = (
        P(("replica", "fsdp"), None),
        P(),
        P("replica", "fsdp", None),
        P("replica", "fsdp", None),
        P("replica", "fsdp", None),
        P("fsdp", "replica"),
        P("fsdp", "replica"),
    )
    out_specs = (
        P(("replica", "fsdp"), None),
        P("fsdp", "replica"),
        P("fsdp", "replica"),
        P("replica", "fsdp", None),
    )
    ny, nz = mesh.shape["fsdp"] // 4, mesh.shape["replica"] // 2
    return jax.shard_map(
        functools.partial(shards, ny, nz), mesh=mesh, in_specs=in_specs, out_specs=out_specs, check_vma=False
    )
```

```python
import functools

import jax
import jax.numpy as jnp
from jax import lax
from jax.experimental import pallas as pl
from jax.experimental.pallas import tpu as pltpu
from jax.sharding import PartitionSpec as P

BLOCK = 128
LANES = 128
MESH = pl.DeviceIdType.MESH
ORDER = (
    "l0", "n0", "G1", "F1", "T1", "e0", "P0", "n1", "X0", "M0", "t0", "l1",
    "G2", "F2", "T2", "P1", "e1", "l2", "M1", "N0", "t1", "e2", "x0", "l3",
    "G3", "P2", "F3", "T3", "e3", "M2", "t2", "M3", "G4", "X1", "F4", "T4",
    "t3", "P3", "M4", "N1", "t4", "X2", "N2", "x1", "w0", "X3", "N3", "X4",
    "x2", "P4", "x3", "N4", "x4", "Z0",
)
F32, BF16 = jnp.float32, jnp.bfloat16


def kernel(
    ny, nz, cut,
    tok_hbm, gain_hbm, w_hbm, codes_hbm, scales_hbm, outer_hbm, mom_hbm,
    keys, outer_out, mom_out, merged,
    tok, gain, codes, scales, outer, mom,
    normed, full, acc, delta, parts, half, avg_blocks, mine,
    local_in, y_send, y_recv, x_send, x_recv, d_send, d_recv,
    z_send, z_recv, g_send, g_recv, h_send, h_recv, near_sem, far_sem,
):
    nk = ny // 2
    rows, columns = full.shape[1], full.shape[2]
    tokens_here, width = tok.shape
    me_r, me_f = lax.axis_index("replica"), lax.axis_index("fsdp")
    z, xh = me_r // 2, me_r % 2
    xl, y, c = me_f // (2 * ny), (me_f // 2) % ny, me_f % 2

    def fsdp(col, row, core):
        return (col * ny + lax.rem(row + 2 * ny, ny)) * 2 + core

    def rep(zz, hh):
        return lax.rem(zz + 2 * nz, nz) * 2 + hh

    up, down = fsdp(xl, y + 1, c), fsdp(xl, y - 1, c)
    across, twin = fsdp(1 - xl, y, c), fsdp(xl, y, 1 - c)

    inputs = [
        pltpu.make_async_copy(w_hbm.at[0], full.at[me_f], local_in.at[0]),
        pltpu.make_async_copy(codes_hbm.at[0], codes, local_in.at[1]),
        pltpu.make_async_copy(scales_hbm, scales, local_in.at[2]),
        pltpu.make_async_copy(outer_hbm, outer, local_in.at[3]),
        pltpu.make_async_copy(mom_hbm, mom, local_in.at[4]),
        pltpu.make_async_copy(gain_hbm, gain, local_in.at[5]),
        pltpu.make_async_copy(tok_hbm, tok, local_in.at[6]),
    ]
    barrier = pltpu.get_barrier_semaphore()
    near = [up, down, across, twin]
    far = [rep(z + j, xh) for j in range(1, nz)] + [rep(z, 1 - xh)]
    odd = lax.rem(xl + y + c, 2) == 1
    late = z >= nz // 2

    @pl.when(odd)
    def _():
        for other in near:
            pl.semaphore_signal(barrier, inc=1, device_id={"fsdp": other, "replica": me_r}, device_id_type=MESH)

    for copy in inputs:
        copy.start()

    @pl.when(jnp.logical_not(odd))
    def _():
        pl.semaphore_wait(barrier, len(near))
        for other in near:
            pl.semaphore_signal(near_sem, inc=1, device_id={"fsdp": other, "replica": me_r}, device_id_type=MESH)

    @pl.when(odd)
    def _():
        pl.semaphore_wait(near_sem, len(near))

    def meet_far():
        @pl.when(odd)
        def _():
            pl.semaphore_wait(barrier, len(far))
            pl.semaphore_signal(far_sem, inc=1, device_id={"fsdp": twin, "replica": me_r}, device_id_type=MESH)

        @pl.when(jnp.logical_not(odd))
        def _():
            pl.semaphore_wait(far_sem, 1)

    FIRST, SECOND, ALL = (0, cut), (cut, rows - cut), (0, rows)
    EVERY = (0, columns)
    HALF = ((0, columns // 2), (columns // 2, columns // 2))

    def region(owner, rr, cc):
        return full.at[owner, pl.ds(rr[0], rr[1]), pl.ds(cc[0], cc[1])]

    def copy_to(target, owner, rr, cc, send, recv, own=False):
        source = region(owner, rr, cc)
        return pltpu.make_async_remote_copy(
            src_ref=source,
            dst_ref=region(owner, rr, cc),
            send_sem=send,
            recv_sem=recv,
            device_id={"fsdp": target, "replica": me_r},
            device_id_type=MESH,
        )

    sent = []

    def start(copy):
        copy.start()
        sent.append(copy)

    toward = (up, down)
    sign = (1, -1)

    def y_copy(d, col, k, part):
        owner = fsdp(col, y - sign[d] * (k - 1), c)
        cc = HALF[d] if k == nk else EVERY
        rr = SECOND if part == 1 else FIRST
        index = (k - 1) * 3 + part
        return copy_to(toward[d], owner, rr, cc, y_send.at[d, index], y_recv.at[d, index], own=(part < 2 and k == 1))

    def y_arrived(d, col, k, part):
        owner = fsdp(col, y - sign[d] * k, c)
        cc = HALF[d] if k == nk else EVERY
        rr = SECOND if part == 1 else FIRST
        index = (k - 1) * 3 + part
        copy_to(toward[d], owner, rr, cc, y_send.at[d, index], y_recv.at[d, index]).wait_recv()

    def x_piece(col, d, k):
        if k == 0:
            return fsdp(col, y, c), (FIRST, SECOND)[d], EVERY, d
        owner = fsdp(col, y - sign[d] * k, c)
        return owner, SECOND, HALF[d] if k == nk else EVERY, 2 * k + d

    def x_copy(d, k):
        owner, rr, cc, index = x_piece(xl, d, k)
        return copy_to(across, owner, rr, cc, x_send.at[index], x_recv.at[index], own=k == 0)

    def x_arrived(d, k):
        owner, rr, cc, index = x_piece(1 - xl, d, k)
        copy_to(across, owner, rr, cc, x_send.at[index], x_recv.at[index]).wait_recv()

    def twin_index(other, d, k):
        return other * ny + (0 if k == 0 else 2 * k - 1 + (d if k < nk else 0))

    def twin_copy(other, d, k):
        col = 1 - xl if other else xl
        index = twin_index(other, d, k)
        return copy_to(twin, fsdp(col, y - sign[d] * k, c), ALL, EVERY, d_send.at[index], d_recv.at[index],
                       own=(other == 0 and k == 0))

    def last_copy(part, core):
        index = 2 * ny - 1 + part
        return copy_to(twin, fsdp(1 - xl, y - nk, core), (FIRST, SECOND)[part], EVERY, d_send.at[index], d_recv.at[index])

    def twin_arrived(other, d, k):
        col = 1 - xl if other else xl
        index = twin_index(other, d, k)
        copy_to(twin, fsdp(col, y - sign[d] * k, 1 - c), ALL, EVERY, d_send.at[index], d_recv.at[index]).wait_recv()

    def multiply(other, k, core, first=False):
        col = 1 - xl if other else xl
        count = 1 if k in (0, nk) else 2

        def one(s, carry):
            owner = fsdp(col, y - (1 - 2 * s) * k, core)
            left = normed[:, pl.ds(pl.multiple_of(owner * rows, rows), rows)]
            product = jnp.dot(left, full[owner], preferred_element_type=F32)
            if first:
                acc[...] = product
            else:
                acc[...] += product
            return carry

        lax.fori_loop(0, count, one, 0)

    inputs[0].wait()
    start(x_copy(0, 0))
    for d in (0, 1):
        start(y_copy(d, xl, 1, 1))
    for d in (0, 1):
        start(y_copy(d, xl, 1, 0))
    start(x_copy(1, 0))
    start(twin_copy(0, 0, 0))

    @pl.when(odd)
    def _():
        for other in far:
            pl.semaphore_signal(barrier, inc=1, device_id={"fsdp": me_f, "replica": other}, device_id_type=MESH)

    share = columns // nz
    inputs[1].wait()
    inputs[2].wait()
    for b in range(columns // BLOCK):
        block = codes[:, b * BLOCK:(b + 1) * BLOCK].astype(F32).T
        delta[b * BLOCK:(b + 1) * BLOCK, :] = (block * scales[b:b + 1, :]).astype(BF16)
    reduce_copies = [
        pltpu.make_async_remote_copy(
            src_ref=delta.at[pl.ds(pl.multiple_of(lax.rem(z + j, nz) * share, share), share), :],
            dst_ref=parts.at[j - 1],
            send_sem=z_send.at[j - 1], recv_sem=z_recv.at[j - 1],
            device_id={"fsdp": me_f, "replica": rep(z + j, xh)}, device_id_type=MESH,
        )
        for j in range(1, nz)
    ]
    sent.extend(reduce_copies)

    def outer_send():
        meet_far()
        for copy in reduce_copies:
            copy.start()


    step_rows = 32
    chunks = width // LANES

    def norm(lo, hi):
        def one(i, carry):
            rr = pl.ds(pl.multiple_of(i * step_rows, step_rows), step_rows)
            squares = jnp.zeros((step_rows, LANES), F32)
            for j in range(chunks):
                v = tok[rr, j * LANES:(j + 1) * LANES].astype(F32)
                squares = squares + v * v
            mean = jnp.sum(squares, axis=1, keepdims=True) * (1.0 / width)
            scale = jnp.broadcast_to(lax.rsqrt(mean + 1e-05), (step_rows, LANES))
            for j in range(chunks):
                v = tok[rr, j * LANES:(j + 1) * LANES].astype(F32)
                normed[rr, j * LANES:(j + 1) * LANES] = (v * scale * gain[j:j + 1, :]).astype(BF16)
            return carry

        lax.fori_loop(lo, hi, one, 0)

    blocks = tokens_here // step_rows
    inputs[3].wait()
    inputs[4].wait()
    inputs[5].wait()
    inputs[6].wait()
    def ways(k):
        return (0, 1) if k < nk else (0,)

    def pass_own(k, part):
        for d in (0, 1):
            y_arrived(d, xl, k, part)
            if k < nk:
                start(y_copy(d, xl, k + 1, part))
        if part == 1:
            for d in (0, 1):
                start(x_copy(d, k))

    def own_to_twin(k):
        for d in ways(k):
            start(twin_copy(0, d, k))

    def pass_first(k):
        for d in (0, 1):
            if k == 0:
                if d == 0:
                    x_arrived(0, 0)
                start(y_copy(d, 1 - xl, 1, 2))
            else:
                y_arrived(d, 1 - xl, k, 2)
                if k < nk:
                    start(y_copy(d, 1 - xl, k + 1, 2))
        if k == nk:
            start(last_copy(0, c))

    def complete(k):
        for d in (0, 1) if k else (1,):
            x_arrived(d, k)
        if k == nk:
            start(last_copy(1, c))
            return
        for d in ways(k) if k else (0,):
            start(twin_copy(1, d, k))

    def take(other, k):
        if other and k == nk:
            for part in (0, 1):
                last_copy(part, 1 - c).wait_recv()
        else:
            for d in ways(k) if k else (0,):
                twin_arrived(other, d, k)
        multiply(other, k, 1 - c)

    n_rep = nz * 2
    slim = columns // n_rep

    def outer_sum():
        for j in range(1, nz):
            pltpu.make_async_remote_copy(
                src_ref=parts.at[j - 1], dst_ref=parts.at[j - 1],
                send_sem=z_send.at[j - 1], recv_sem=z_recv.at[j - 1],
                device_id={"fsdp": me_f, "replica": rep(z + j, xh)}, device_id_type=MESH,
            ).wait_recv()

        def total(which):
            lo = pl.multiple_of(z * share + which * slim, slim)
            value = delta[pl.ds(lo, slim), :].astype(F32)
            for j in range(1, nz):
                value = value + parts[j - 1, pl.ds(pl.multiple_of(which * slim, slim), slim), :].astype(F32)
            return value

        half[0] = total(1 - xh).astype(BF16)
        half_copy().start()
        mine[...] = total(xh)

    def half_copy():
        return pltpu.make_async_remote_copy(
            src_ref=half.at[0], dst_ref=half.at[1], send_sem=h_send.at[0], recv_sem=h_recv.at[0],
            device_id={"fsdp": me_f, "replica": rep(z, 1 - xh)}, device_id_type=MESH,
        )

    def slim_copy(owner):
        ref = avg_blocks.at[pl.ds(pl.multiple_of(owner * slim, slim), slim), :]
        return pltpu.make_async_remote_copy(
            src_ref=ref, dst_ref=ref, send_sem=h_send.at[1], recv_sem=h_recv.at[1],
            device_id={"fsdp": me_f, "replica": rep(z, 1 - xh)}, device_id_type=MESH,
        )

    def share_copy(owner_z, j):
        ref = avg_blocks.at[pl.ds(pl.multiple_of(owner_z * share, share), share), :]
        return pltpu.make_async_remote_copy(
            src_ref=ref, dst_ref=ref, send_sem=g_send.at[j - 1], recv_sem=g_recv.at[j - 1],
            device_id={"fsdp": me_f, "replica": rep(z + j, xh)}, device_id_type=MESH,
        )

    slim_out = slim_copy(me_r)
    sent.extend([half_copy(), slim_out])

    def outer_step():
        half_copy().wait_recv()
        average = (mine[...] + half[1].astype(F32)) * (1.0 / n_rep)
        moment = 0.9 * mom[...] + average
        stepped = outer[...] - 0.7 * (average + 0.9 * moment)
        mom_out[...] = moment
        outer_out[...] = stepped
        avg_blocks[pl.ds(pl.multiple_of(me_r * slim, slim), slim), :] = stepped.astype(BF16)
        slim_out.start()

    spread_copies = [share_copy(z, j) for j in range(1, nz)]

    def outer_spread():
        slim_copy(rep(z, 1 - xh)).wait_recv()
        for copy in spread_copies:
            copy.start()

    def outer_merge():
        for j in range(1, nz):
            share_copy(lax.rem(z - j + nz, nz), j).wait_recv()
        for b in range(columns // LANES):
            block = avg_blocks[b * LANES:(b + 1) * LANES, :].astype(F32).T
            own = full[me_f, :, b * LANES:(b + 1) * LANES].astype(F32)
            merged[0, :, b * LANES:(b + 1) * LANES] = (0.5 * own + 0.5 * block).astype(BF16)

    def settle():
        for copy in sent:
            copy.wait_send()
        sent.clear()

    early = jnp.logical_not(late)
    steps = {
        "F": lambda k: pass_own(k, 0),
        "G": lambda k: pass_own(k, 1),
        "T": own_to_twin,
        "P": pass_first,
        "X": complete,
        "M": lambda k: multiply(0, k, c, first=k == 0),
        "N": lambda k: multiply(1, k, c),
        "t": lambda k: take(0, k),
        "x": lambda k: take(1, k),
        "n": lambda k: norm(blocks * k // 2, blocks * (k + 1) // 2),
        "e": lambda k: pl.when(early)((outer_send, outer_sum, outer_step, outer_spread)[k]),
        "l": lambda k: pl.when(late)((outer_send, outer_sum, outer_step, outer_spread)[k]),
        "Z": lambda k: outer_merge(),
        "w": lambda k: settle(),
    }
    for step in ORDER:
        steps[step[0]](int(step[1]))
    sent.extend(spread_copies)
    keys[...] = acc[...].astype(BF16)
    settle()


def write(keys, outer, mom, merged, keys_out, outer_out, mom_out, merged_out, sems):
    pairs = ((keys, keys_out), (outer, outer_out), (mom, mom_out), (merged, merged_out))
    copies = [pltpu.make_async_copy(a, b, sems.at[i]) for i, (a, b) in enumerate(pairs)]
    for copy in copies:
        copy.start()
    for copy in copies:
        copy.wait()


def shards(ny, nz, tokens, norm_gain, weights, codes, scales, outer, momentum):
    tokens_here, width = tokens.shape
    _, rows, columns = weights.shape
    n_fsdp, n_rep = 4 * ny, 2 * nz
    slim, share = columns // n_rep, columns // nz
    nk = ny // 2
    cut = rows * 7 // 16
    hbm = pl.BlockSpec(memory_space=pltpu.HBM)
    vmem = pl.BlockSpec(memory_space=pltpu.VMEM)
    dma = pltpu.SemaphoreType.DMA
    results = (
        ((tokens_here, columns), BF16),
        ((slim, rows), F32),
        ((slim, rows), F32),
        ((1, rows, columns), BF16),
    )
    held = pl.pallas_call(
        functools.partial(kernel, ny, nz, cut),
        out_shape=tuple(pltpu.VMEM(shape, dtype) for shape, dtype in results),
        in_specs=[hbm] * 7,
        out_specs=(vmem,) * 4,
        scratch_shapes=[
            pltpu.VMEM((tokens_here, width), BF16),
            pltpu.VMEM((width // LANES, LANES), F32),
            pltpu.VMEM((rows, columns), BF16),
            pltpu.VMEM((columns // BLOCK, rows), F32),
            pltpu.VMEM((slim, rows), F32),
            pltpu.VMEM((slim, rows), F32),
            pltpu.VMEM((tokens_here, width), BF16),
            pltpu.VMEM((n_fsdp, rows, columns), BF16),
            pltpu.VMEM((tokens_here, columns), F32),
            pltpu.VMEM((columns, rows), BF16),
            pltpu.VMEM((nz - 1, share, rows), BF16),
            pltpu.VMEM((2, slim, rows), BF16),
            pltpu.VMEM((columns, rows), BF16),
            pltpu.VMEM((slim, rows), F32),
            dma((7,)),
            dma((2, 3 * nk)), dma((2, 3 * nk)),
            dma((2 * nk + 2,)), dma((2 * nk + 2,)),
            dma((2 * ny + 1,)), dma((2 * ny + 1,)),
            dma((nz - 1,)), dma((nz - 1,)),
            dma((nz - 1,)), dma((nz - 1,)),
            dma((2,)), dma((2,)),
            pltpu.SemaphoreType.REGULAR, pltpu.SemaphoreType.REGULAR,
        ],
        compiler_params=pltpu.CompilerParams(
            collective_id=0, has_side_effects=True, vmem_limit_bytes=60 * 1024 * 1024
        ),
        cost_estimate=pl.CostEstimate(
            flops=2 * tokens_here * width * columns, bytes_accessed=2 * tokens_here * width, transcendentals=0
        ),
    )(
        tokens,
        norm_gain.reshape(width // LANES, LANES),
        weights,
        codes,
        scales[0].T,
        outer.T,
        momentum.T,
    )
    keys, outer_next, moment_next, merged = pl.pallas_call(
        write,
        out_shape=tuple(jax.ShapeDtypeStruct(shape, dtype) for shape, dtype in results),
        in_specs=[vmem] * 4,
        out_specs=(hbm,) * 4,
        scratch_shapes=[dma((4,))],
        compiler_params=pltpu.CompilerParams(vmem_limit_bytes=4 * 1024 * 1024),
    )(*held)
    return keys, outer_next.T, moment_next.T, merged


def solution(mesh):
    in_specs = (
        P(("replica", "fsdp"), None),
        P(),
        P("replica", "fsdp", None),
        P("replica", "fsdp", None),
        P("replica", "fsdp", None),
        P("fsdp", "replica"),
        P("fsdp", "replica"),
    )
    out_specs = (
        P(("replica", "fsdp"), None),
        P("fsdp", "replica"),
        P("fsdp", "replica"),
        P("replica", "fsdp", None),
    )
    ny, nz = mesh.shape["fsdp"] // 4, mesh.shape["replica"] // 2
    return jax.shard_map(
        functools.partial(shards, ny, nz), mesh=mesh, in_specs=in_specs, out_specs=out_specs, check_vma=False
    )
```

```python
import functools

import jax
import jax.numpy as jnp
from jax import lax
from jax.experimental import pallas as pl
from jax.experimental.pallas import tpu as pltpu
from jax.sharding import PartitionSpec as P

BLOCK = 128
LANES = 128
MESH = pl.DeviceIdType.MESH
ORDER = (
    "l0", "n0", "G1", "F1", "T1", "e0", "P0", "n1", "X0", "M0", "t0", "l1",
    "G2", "F2", "T2", "P1", "e1", "l2", "M1", "N0", "t1", "e2", "x0", "l3",
    "G3", "P2", "F3", "T3", "e3", "M2", "t2", "M3", "G4", "X1", "F4", "T4",
    "t3", "P3", "M4", "N1", "t4", "X2", "N2", "x1", "w0", "X3", "N3", "X4",
    "x2", "P4", "x3", "N4", "x4", "Z0",
)
F32, BF16 = jnp.float32, jnp.bfloat16


def kernel(
    ny, nz, cut,
    tok_hbm, gain_hbm, w_hbm, codes_hbm, scales_hbm, outer_hbm, mom_hbm,
    keys, outer_out, mom_out, merged,
    tok, gain, codes, scales, outer, mom,
    normed, full, acc, delta, parts, half, avg_blocks, mine,
    local_in, y_send, y_recv, x_send, x_recv, d_send, d_recv,
    z_send, z_recv, g_send, g_recv, h_send, h_recv, near_sem, far_sem,
):
    nk = ny // 2
    rows, columns = full.shape[1], full.shape[2]
    tokens_here, width = tok.shape
    me_r, me_f = lax.axis_index("replica"), lax.axis_index("fsdp")
    z, xh = me_r // 2, me_r % 2
    xl, y, c = me_f // (2 * ny), (me_f // 2) % ny, me_f % 2

    def fsdp(col, row, core):
        return (col * ny + lax.rem(row + 2 * ny, ny)) * 2 + core

    def rep(zz, hh):
        return lax.rem(zz + 2 * nz, nz) * 2 + hh

    up, down = fsdp(xl, y + 1, c), fsdp(xl, y - 1, c)
    across, twin = fsdp(1 - xl, y, c), fsdp(xl, y, 1 - c)

    inputs = [
        pltpu.make_async_copy(w_hbm.at[0], full.at[me_f], local_in.at[0]),
        pltpu.make_async_copy(codes_hbm.at[0], codes, local_in.at[1]),
        pltpu.make_async_copy(scales_hbm, scales, local_in.at[2]),
        pltpu.make_async_copy(outer_hbm, outer, local_in.at[3]),
        pltpu.make_async_copy(mom_hbm, mom, local_in.at[4]),
        pltpu.make_async_copy(gain_hbm, gain, local_in.at[5]),
        pltpu.make_async_copy(tok_hbm, tok, local_in.at[6]),
    ]
    barrier = pltpu.get_barrier_semaphore()
    near = [up, down, across, twin]
    far = [rep(z + j, xh) for j in range(1, nz)] + [rep(z, 1 - xh)]
    odd = lax.rem(xl + y + c, 2) == 1
    late = z >= nz // 2

    @pl.when(odd)
    def _():
        for other in near:
            pl.semaphore_signal(barrier, inc=1, device_id={"fsdp": other, "replica": me_r}, device_id_type=MESH)

    for copy in inputs:
        copy.start()

    @pl.when(jnp.logical_not(odd))
    def _():
        pl.semaphore_wait(barrier, len(near))
        for other in near:
            pl.semaphore_signal(near_sem, inc=1, device_id={"fsdp": other, "replica": me_r}, device_id_type=MESH)

    @pl.when(odd)
    def _():
        pl.semaphore_wait(near_sem, len(near))

    def meet_far():
        @pl.when(odd)
        def _():
            pl.semaphore_wait(barrier, len(far))
            pl.semaphore_signal(far_sem, inc=1, device_id={"fsdp": twin, "replica": me_r}, device_id_type=MESH)

        @pl.when(jnp.logical_not(odd))
        def _():
            pl.semaphore_wait(far_sem, 1)

    FIRST, SECOND, ALL = (0, cut), (cut, rows - cut), (0, rows)
    EVERY = (0, columns)
    HALF = ((0, columns // 2), (columns // 2, columns // 2))

    def region(owner, rr, cc):
        return full.at[owner, pl.ds(rr[0], rr[1]), pl.ds(cc[0], cc[1])]

    def copy_to(target, owner, rr, cc, send, recv, own=False):
        source = region(owner, rr, cc)
        return pltpu.make_async_remote_copy(
            src_ref=source,
            dst_ref=region(owner, rr, cc),
            send_sem=send,
            recv_sem=recv,
            device_id={"fsdp": target, "replica": me_r},
            device_id_type=MESH,
        )

    sent = []

    def start(copy):
        copy.start()
        sent.append(copy)

    toward = (up, down)
    sign = (1, -1)

    def y_copy(d, col, k, part):
        owner = fsdp(col, y - sign[d] * (k - 1), c)
        cc = HALF[d] if k == nk else EVERY
        rr = SECOND if part == 1 else FIRST
        index = (k - 1) * 3 + part
        return copy_to(toward[d], owner, rr, cc, y_send.at[d, index], y_recv.at[d, index], own=(part < 2 and k == 1))

    def y_arrived(d, col, k, part):
        owner = fsdp(col, y - sign[d] * k, c)
        cc = HALF[d] if k == nk else EVERY
        rr = SECOND if part == 1 else FIRST
        index = (k - 1) * 3 + part
        copy_to(toward[d], owner, rr, cc, y_send.at[d, index], y_recv.at[d, index]).wait_recv()

    def x_piece(col, d, k):
        if k == 0:
            return fsdp(col, y, c), (FIRST, SECOND)[d], EVERY, d
        owner = fsdp(col, y - sign[d] * k, c)
        return owner, SECOND, HALF[d] if k == nk else EVERY, 2 * k + d

    def x_copy(d, k):
        owner, rr, cc, index = x_piece(xl, d, k)
        return copy_to(across, owner, rr, cc, x_send.at[index], x_recv.at[index], own=k == 0)

    def x_arrived(d, k):
        owner, rr, cc, index = x_piece(1 - xl, d, k)
        copy_to(across, owner, rr, cc, x_send.at[index], x_recv.at[index]).wait_recv()

    def twin_index(other, d, k):
        return other * ny + (0 if k == 0 else 2 * k - 1 + (d if k < nk else 0))

    def twin_copy(other, d, k):
        col = 1 - xl if other else xl
        index = twin_index(other, d, k)
        return copy_to(twin, fsdp(col, y - sign[d] * k, c), ALL, EVERY, d_send.at[index], d_recv.at[index],
                       own=(other == 0 and k == 0))

    def last_copy(part, core):
        index = 2 * ny - 1 + part
        return copy_to(twin, fsdp(1 - xl, y - nk, core), (FIRST, SECOND)[part], EVERY, d_send.at[index], d_recv.at[index])

    def twin_arrived(other, d, k):
        col = 1 - xl if other else xl
        index = twin_index(other, d, k)
        copy_to(twin, fsdp(col, y - sign[d] * k, 1 - c), ALL, EVERY, d_send.at[index], d_recv.at[index]).wait_recv()

    def multiply(other, k, core, first=False):
        col = 1 - xl if other else xl
        count = 1 if k in (0, nk) else 2

        def one(s, carry):
            owner = fsdp(col, y - (1 - 2 * s) * k, core)
            left = normed[:, pl.ds(pl.multiple_of(owner * rows, rows), rows)]
            product = jnp.dot(left, full[owner], preferred_element_type=F32)
            if first:
                acc[...] = product
            else:
                acc[...] += product
            return carry

        lax.fori_loop(0, count, one, 0)

    inputs[0].wait()
    start(x_copy(0, 0))
    for d in (0, 1):
        start(y_copy(d, xl, 1, 1))
    start(x_copy(1, 0))
    for d in (0, 1):
        start(y_copy(d, xl, 1, 0))
    start(twin_copy(0, 0, 0))

    @pl.when(odd)
    def _():
        for other in far:
            pl.semaphore_signal(barrier, inc=1, device_id={"fsdp": me_f, "replica": other}, device_id_type=MESH)

    share = columns // nz
    inputs[1].wait()
    inputs[2].wait()
    for b in range(columns // BLOCK):
        block = codes[:, b * BLOCK:(b + 1) * BLOCK].astype(F32).T
        delta[b * BLOCK:(b + 1) * BLOCK, :] = (block * scales[b:b + 1, :]).astype(BF16)
    reduce_copies = [
        pltpu.make_async_remote_copy(
            src_ref=delta.at[pl.ds(pl.multiple_of(lax.rem(z + j, nz) * share, share), share), :],
            dst_ref=parts.at[j - 1],
            send_sem=z_send.at[j - 1], recv_sem=z_recv.at[j - 1],
            device_id={"fsdp": me_f, "replica": rep(z + j, xh)}, device_id_type=MESH,
        )
        for j in range(1, nz)
    ]
    sent.extend(reduce_copies)

    def outer_send():
        meet_far()
        for copy in reduce_copies:
            copy.start()


    step_rows = 32
    chunks = width // LANES

    def norm(lo, hi):
        def one(i, carry):
            rr = pl.ds(pl.multiple_of(i * step_rows, step_rows), step_rows)
            squares = jnp.zeros((step_rows, LANES), F32)
            for j in range(chunks):
                v = tok[rr, j * LANES:(j + 1) * LANES].astype(F32)
                squares = squares + v * v
            mean = jnp.sum(squares, axis=1, keepdims=True) * (1.0 / width)
            scale = jnp.broadcast_to(lax.rsqrt(mean + 1e-05), (step_rows, LANES))
            for j in range(chunks):
                v = tok[rr, j * LANES:(j + 1) * LANES].astype(F32)
                normed[rr, j * LANES:(j + 1) * LANES] = (v * scale * gain[j:j + 1, :]).astype(BF16)
            return carry

        lax.fori_loop(lo, hi, one, 0)

    blocks = tokens_here // step_rows
    inputs[3].wait()
    inputs[4].wait()
    inputs[5].wait()
    inputs[6].wait()
    def ways(k):
        return (0, 1) if k < nk else (0,)

    def pass_own(k, part):
        for d in (0, 1):
            y_arrived(d, xl, k, part)
            if k < nk:
                start(y_copy(d, xl, k + 1, part))
        if part == 1:
            for d in (0, 1):
                start(x_copy(d, k))

    def own_to_twin(k):
        for d in ways(k):
            start(twin_copy(0, d, k))

    def pass_first(k):
        for d in (0, 1):
            if k == 0:
                if d == 0:
                    x_arrived(0, 0)
                start(y_copy(d, 1 - xl, 1, 2))
            else:
                y_arrived(d, 1 - xl, k, 2)
                if k < nk:
                    start(y_copy(d, 1 - xl, k + 1, 2))
        if k == nk:
            start(last_copy(0, c))

    def complete(k):
        for d in (0, 1) if k else (1,):
            x_arrived(d, k)
        if k == nk:
            start(last_copy(1, c))
            return
        for d in ways(k) if k else (0,):
            start(twin_copy(1, d, k))

    def take(other, k):
        if other and k == nk:
            for part in (0, 1):
                last_copy(part, 1 - c).wait_recv()
        else:
            for d in ways(k) if k else (0,):
                twin_arrived(other, d, k)
        multiply(other, k, 1 - c)

    n_rep = nz * 2
    slim = columns // n_rep

    def outer_sum():
        for j in range(1, nz):
            pltpu.make_async_remote_copy(
                src_ref=parts.at[j - 1], dst_ref=parts.at[j - 1],
                send_sem=z_send.at[j - 1], recv_sem=z_recv.at[j - 1],
                device_id={"fsdp": me_f, "replica": rep(z + j, xh)}, device_id_type=MESH,
            ).wait_recv()

        def total(which):
            lo = pl.multiple_of(z * share + which * slim, slim)
            value = delta[pl.ds(lo, slim), :].astype(F32)
            for j in range(1, nz):
                value = value + parts[j - 1, pl.ds(pl.multiple_of(which * slim, slim), slim), :].astype(F32)
            return value

        half[0] = total(1 - xh).astype(BF16)
        half_copy().start()
        mine[...] = total(xh)

    def half_copy():
        return pltpu.make_async_remote_copy(
            src_ref=half.at[0], dst_ref=half.at[1], send_sem=h_send.at[0], recv_sem=h_recv.at[0],
            device_id={"fsdp": me_f, "replica": rep(z, 1 - xh)}, device_id_type=MESH,
        )

    def slim_copy(owner):
        ref = avg_blocks.at[pl.ds(pl.multiple_of(owner * slim, slim), slim), :]
        return pltpu.make_async_remote_copy(
            src_ref=ref, dst_ref=ref, send_sem=h_send.at[1], recv_sem=h_recv.at[1],
            device_id={"fsdp": me_f, "replica": rep(z, 1 - xh)}, device_id_type=MESH,
        )

    def share_copy(owner_z, j):
        ref = avg_blocks.at[pl.ds(pl.multiple_of(owner_z * share, share), share), :]
        return pltpu.make_async_remote_copy(
            src_ref=ref, dst_ref=ref, send_sem=g_send.at[j - 1], recv_sem=g_recv.at[j - 1],
            device_id={"fsdp": me_f, "replica": rep(z + j, xh)}, device_id_type=MESH,
        )

    slim_out = slim_copy(me_r)
    sent.extend([half_copy(), slim_out])

    def outer_step():
        half_copy().wait_recv()
        average = (mine[...] + half[1].astype(F32)) * (1.0 / n_rep)
        moment = 0.9 * mom[...] + average
        stepped = outer[...] - 0.7 * (average + 0.9 * moment)
        mom_out[...] = moment
        outer_out[...] = stepped
        avg_blocks[pl.ds(pl.multiple_of(me_r * slim, slim), slim), :] = stepped.astype(BF16)
        slim_out.start()

    spread_copies = [share_copy(z, j) for j in range(1, nz)]

    def outer_spread():
        slim_copy(rep(z, 1 - xh)).wait_recv()
        for copy in spread_copies:
            copy.start()

    def outer_merge():
        for j in range(1, nz):
            share_copy(lax.rem(z - j + nz, nz), j).wait_recv()
        for b in range(columns // LANES):
            block = avg_blocks[b * LANES:(b + 1) * LANES, :].astype(F32).T
            own = full[me_f, :, b * LANES:(b + 1) * LANES].astype(F32)
            merged[0, :, b * LANES:(b + 1) * LANES] = (0.5 * own + 0.5 * block).astype(BF16)

    def settle():
        for copy in sent:
            copy.wait_send()
        sent.clear()

    early = jnp.logical_not(late)
    steps = {
        "F": lambda k: pass_own(k, 0),
        "G": lambda k: pass_own(k, 1),
        "T": own_to_twin,
        "P": pass_first,
        "X": complete,
        "M": lambda k: multiply(0, k, c, first=k == 0),
        "N": lambda k: multiply(1, k, c),
        "t": lambda k: take(0, k),
        "x": lambda k: take(1, k),
        "n": lambda k: norm(blocks * k // 2, blocks * (k + 1) // 2),
        "e": lambda k: pl.when(early)((outer_send, outer_sum, outer_step, outer_spread)[k]),
        "l": lambda k: pl.when(late)((outer_send, outer_sum, outer_step, outer_spread)[k]),
        "Z": lambda k: outer_merge(),
        "w": lambda k: settle(),
    }
    for step in ORDER:
        steps[step[0]](int(step[1]))
    sent.extend(spread_copies)
    keys[...] = acc[...].astype(BF16)
    settle()


def write(keys, outer, mom, merged, keys_out, outer_out, mom_out, merged_out, sems):
    pairs = ((keys, keys_out), (outer, outer_out), (mom, mom_out), (merged, merged_out))
    copies = [pltpu.make_async_copy(a, b, sems.at[i]) for i, (a, b) in enumerate(pairs)]
    for copy in copies:
        copy.start()
    for copy in copies:
        copy.wait()


def shards(ny, nz, tokens, norm_gain, weights, codes, scales, outer, momentum):
    tokens_here, width = tokens.shape
    _, rows, columns = weights.shape
    n_fsdp, n_rep = 4 * ny, 2 * nz
    slim, share = columns // n_rep, columns // nz
    nk = ny // 2
    cut = rows * 7 // 16
    hbm = pl.BlockSpec(memory_space=pltpu.HBM)
    vmem = pl.BlockSpec(memory_space=pltpu.VMEM)
    dma = pltpu.SemaphoreType.DMA
    results = (
        ((tokens_here, columns), BF16),
        ((slim, rows), F32),
        ((slim, rows), F32),
        ((1, rows, columns), BF16),
    )
    held = pl.pallas_call(
        functools.partial(kernel, ny, nz, cut),
        out_shape=tuple(pltpu.VMEM(shape, dtype) for shape, dtype in results),
        in_specs=[hbm] * 7,
        out_specs=(vmem,) * 4,
        scratch_shapes=[
            pltpu.VMEM((tokens_here, width), BF16),
            pltpu.VMEM((width // LANES, LANES), F32),
            pltpu.VMEM((rows, columns), BF16),
            pltpu.VMEM((columns // BLOCK, rows), F32),
            pltpu.VMEM((slim, rows), F32),
            pltpu.VMEM((slim, rows), F32),
            pltpu.VMEM((tokens_here, width), BF16),
            pltpu.VMEM((n_fsdp, rows, columns), BF16),
            pltpu.VMEM((tokens_here, columns), F32),
            pltpu.VMEM((columns, rows), BF16),
            pltpu.VMEM((nz - 1, share, rows), BF16),
            pltpu.VMEM((2, slim, rows), BF16),
            pltpu.VMEM((columns, rows), BF16),
            pltpu.VMEM((slim, rows), F32),
            dma((7,)),
            dma((2, 3 * nk)), dma((2, 3 * nk)),
            dma((2 * nk + 2,)), dma((2 * nk + 2,)),
            dma((2 * ny + 1,)), dma((2 * ny + 1,)),
            dma((nz - 1,)), dma((nz - 1,)),
            dma((nz - 1,)), dma((nz - 1,)),
            dma((2,)), dma((2,)),
            pltpu.SemaphoreType.REGULAR, pltpu.SemaphoreType.REGULAR,
        ],
        compiler_params=pltpu.CompilerParams(
            collective_id=0, has_side_effects=True, vmem_limit_bytes=60 * 1024 * 1024
        ),
        cost_estimate=pl.CostEstimate(
            flops=2 * tokens_here * width * columns, bytes_accessed=2 * tokens_here * width, transcendentals=0
        ),
    )(
        tokens,
        norm_gain.reshape(width // LANES, LANES),
        weights,
        codes,
        scales[0].T,
        outer.T,
        momentum.T,
    )
    keys, outer_next, moment_next, merged = pl.pallas_call(
        write,
        out_shape=tuple(jax.ShapeDtypeStruct(shape, dtype) for shape, dtype in results),
        in_specs=[vmem] * 4,
        out_specs=(hbm,) * 4,
        scratch_shapes=[dma((4,))],
        compiler_params=pltpu.CompilerParams(vmem_limit_bytes=4 * 1024 * 1024),
    )(*held)
    return keys, outer_next.T, moment_next.T, merged


def solution(mesh):
    in_specs = (
        P(("replica", "fsdp"), None),
        P(),
        P("replica", "fsdp", None),
        P("replica", "fsdp", None),
        P("replica", "fsdp", None),
        P("fsdp", "replica"),
        P("fsdp", "replica"),
    )
    out_specs = (
        P(("replica", "fsdp"), None),
        P("fsdp", "replica"),
        P("fsdp", "replica"),
        P("replica", "fsdp", None),
    )
    ny, nz = mesh.shape["fsdp"] // 4, mesh.shape["replica"] // 2
    return jax.shard_map(
        functools.partial(shards, ny, nz), mesh=mesh, in_specs=in_specs, out_specs=out_specs, check_vma=False
    )
```
